1024 devices in a mesh: feat: 16 (over z), dp: 64 (over y, x, core).
Axes of the slice: x: 4, y: 8, z: 16, core: 2. Of those that a mesh axis runs over, the one named last changes fastest.
Arguments:
- targets_x: bfloat16 [1024, 131072], P('feat', 'dp'), may hold values from -6 to 6
- frontier: bfloat16 [1024, 393216], P('feat', 'dp'), may hold values from -6 to 6
- neighbours1: int32 [10, 131072], P(None, 'dp'), may hold values from 0 to 6143
- counts1: int32 [131072], P('dp'), may hold values from 1 to 10
- w1_self: bfloat16 [1024, 256], P('feat'), may hold values from -0.125 to 0.125
- w1_neigh: bfloat16 [1024, 256], P('feat'), may hold values from -0.1875 to 0.1875
- history: bfloat16 [524288, 256], P(('dp', 'feat')), may hold values from -6 to 6
- neighbours2: int32 [25, 131072], P(None, ('dp', 'feat')), may hold values from 0 to 511
- counts2: int32 [131072], P(('dp', 'feat')), may hold values from 1 to 25
- w2_self: bfloat16 [256, 256], replicated, may hold values from -0.375 to 0.375
- w2_neigh: bfloat16 [256, 256], replicated, may hold values from -0.375 to 0.375
- out_grad: bfloat16 [131072, 256], P(('dp', 'feat')), may hold values from -6 to 6
Outputs:
- logits: bfloat16 [131072, 256], P(('dp', 'feat'))
- grad_w1_self: float32 [1024, 256], P('feat')
- grad_w1_neigh: float32 [1024, 256], P('feat')
- grad_w2_self: float32 [256, 256], replicated
- grad_w2_neigh: float32 [256, 256], replicated
The draws below stay inside these ranges and needn't reach their ends.
All inputs are finite; a program needn't handle non-finite values.
Results may differ from the reference program's by a relative error of at most 0.0051.
Values may be sent and summed in bfloat16 or wider, within the bound.
A program may use at most 32 MiB of HBM per device.

```python
import jax
import jax.numpy as jnp
from jax import lax

F_IN = 1024
H = 256
FANOUT1 = 10
FANOUT2 = 25
TGT_DEV = 128
HIST_DEV = 512
GROUP = 2048
FR_GRP = 6144
TARGETS = 131072
FRONTIER = 393216
HIST = 524288
N_FEAT = 16
N_DP = 64


def plant(drawn, stream_key, least, largest):
    index_at = [jax.random.randint(jax.random.fold_in(stream_key, axis), (), 0, length) for axis, length in enumerate(drawn.shape)]
    longest = drawn.shape.index(max(drawn.shape))
    beside = index_at[:longest] + [(index_at[longest] + 1) % drawn.shape[longest]] + index_at[longest + 1:]
    return drawn.at[tuple(index_at)].set(least).at[tuple(beside)].set(largest)


def levels(rng, shape, pieces, least, top_value):
    gain, own = 1.0, jax.random.fold_in(rng, 6)
    for dim, shards_of in pieces:
        steps = jnp.exp(jax.random.uniform(jax.random.fold_in(own, dim), (shards_of,), jnp.float32, least / len(pieces), top_value / len(pieces)))
        gain = gain * jnp.repeat(steps, shape[dim] // shards_of).reshape([-1 if axis == dim else 1 for axis in range(len(shape))])
    return gain


def centred(own_key, shape, scale, reach, cuts=(), dtype=jnp.bfloat16):
    entries = jax.random.normal(own_key, shape, jnp.float32) * scale
    if len(cuts) > 0:
        entries = levels(own_key, shape, cuts, -0.22, 0.18) * entries
    return jnp.clip(entries, min=-reach, max=reach).astype(dtype)


def setup_inputs(seed: int = 0) -> dict:
    keys = jax.random.split(jax.random.key(seed), 13)
    targets_x = centred(keys[0], (F_IN, TARGETS), 1.0, 6.0, ((0, 16), (1, 64)))
    frontier = centred(keys[1], (F_IN, FRONTIER), 1.0, 6.0, ((0, 16), (1, 64)))
    neighbours1 = plant(jax.random.randint(keys[2], (FANOUT1, TARGETS), 0, FR_GRP), jax.random.fold_in(keys[2], 1), 0, FR_GRP - 1).astype(jnp.int32)
    counts1 = plant(jax.random.randint(keys[3], (TARGETS,), 1, FANOUT1 + 1), jax.random.fold_in(keys[3], 1), 1, FANOUT1).astype(jnp.int32)
    w1_self = centred(keys[4], (F_IN, H), (2 * F_IN) ** -0.5, 0.125, ((0, 16),))
    w1_neigh = centred(keys[5], (F_IN, H), F_IN ** -0.5, 0.1875, ((0, 16),))
    history = centred(keys[6], (HIST, H), 1.0, 6.0, ((0, 1024),))
    neighbours2 = plant(jax.random.randint(keys[7], (FANOUT2, TARGETS), 0, HIST_DEV), jax.random.fold_in(keys[7], 1), 0, HIST_DEV - 1).astype(jnp.int32)
    counts2 = plant(jax.random.randint(keys[8], (TARGETS,), 1, FANOUT2 + 1), jax.random.fold_in(keys[8], 1), 1, FANOUT2).astype(jnp.int32)
    w2_self = centred(keys[9], (H, H), H ** -0.5, 0.375)
    w2_neigh = centred(keys[10], (H, H), H ** -0.5, 0.375)
    out_grad = centred(keys[11], (TARGETS, H), 1.0, 6.0, ((0, 1024),))
    return dict(targets_x=targets_x, frontier=frontier, neighbours1=neighbours1, counts1=counts1, w1_self=w1_self, w1_neigh=w1_neigh, history=history, neighbours2=neighbours2, counts2=counts2, w2_self=w2_self, w2_neigh=w2_neigh, out_grad=out_grad)


def mean_rows(lookup, row_ids, counts):
    picked = lookup[row_ids]
    usable = lax.broadcasted_iota(jnp.int32, row_ids.shape, 1) < counts[:, None]
    summed = jnp.sum(jnp.where(usable[:, :, None], picked.astype(jnp.float32), jnp.float32(0.0)), axis=1)
    return (summed / counts[:, None].astype(jnp.float32)).astype(jnp.bfloat16)


def group_mean(blocks):
    return mean_rows(blocks[0], blocks[1], blocks[2])


def silu_slope(pre_act):
    sigmoid_val = jax.nn.sigmoid(pre_act)
    return sigmoid_val * (1.0 + pre_act * (1.0 - sigmoid_val))


def reference(targets_x, frontier, neighbours1, counts1, w1_self, w1_neigh, history, neighbours2, counts2, w2_self, w2_neigh, out_grad):
    rows_x = targets_x.T
    agg_one = lax.map(group_mean, (frontier.T.reshape(N_DP, FR_GRP, F_IN), neighbours1.T.reshape(N_DP, GROUP, FANOUT1), counts1.reshape(N_DP, GROUP))).reshape(TARGETS, F_IN)
    pre_act = jnp.dot(rows_x, w1_self, preferred_element_type=jnp.float32) + jnp.dot(agg_one, w1_neigh, preferred_element_type=jnp.float32)
    hidden = jax.nn.silu(pre_act).astype(jnp.bfloat16)
    blocks_all = N_DP * N_FEAT
    agg_two = lax.map(group_mean, (history.reshape(blocks_all, HIST_DEV, H), neighbours2.T.reshape(blocks_all, TGT_DEV, FANOUT2), counts2.reshape(blocks_all, TGT_DEV))).reshape(TARGETS, H)
    logits = (jnp.dot(hidden, w2_self, preferred_element_type=jnp.float32) + jnp.dot(agg_two, w2_neigh, preferred_element_type=jnp.float32)).astype(jnp.bfloat16)
    grad_w2_self = jnp.dot(hidden.T, out_grad, preferred_element_type=jnp.float32)
    grad_w2_neigh = jnp.dot(agg_two.T, out_grad, preferred_element_type=jnp.float32)
    back = jnp.dot(out_grad, w2_self.T, preferred_element_type=jnp.float32)
    pre_grad = (back * silu_slope(pre_act)).astype(jnp.bfloat16)
    grad_w1_self = jnp.dot(targets_x, pre_grad, preferred_element_type=jnp.float32)
    grad_w1_neigh = jnp.dot(agg_one.T, pre_grad, preferred_element_type=jnp.float32)
    return logits, grad_w1_self, grad_w1_neigh, grad_w2_self, grad_w2_neigh
```

```python
import functools

import jax
import jax.numpy as jnp
from jax import lax
from jax.experimental import pallas as pl
from jax.experimental.pallas import tpu as pltpu
from jax.sharding import PartitionSpec as P

MESH = pl.DeviceIdType.MESH
F32, BF16 = jnp.float32, jnp.bfloat16


def dot(left, right):
    return jnp.dot(left, right, preferred_element_type=F32)


def dot_rows(left, right):
    return lax.dot_general(left, right, (((0,), (0,)), ((), ())), preferred_element_type=F32)


def gather_kernel(
    slots, unroll, idx_ref, cnt_ref, f_ref, tx_ref, hist_ref, n2_ref, c2_ref,
    x_ref, xt_ref, a2_ref, tab, rows,
):
    width, nodes = f_ref.shape
    targets = tx_ref.shape[1]
    tab[nodes : nodes + 8, :] = jnp.zeros((8, 128), F32)

    def turn(i, carry):
        at = pl.multiple_of(i * 128, 128)
        tab[pl.ds(at, 128), 0:width] = f_ref[:, pl.ds(at, 128)].astype(F32).T
        return carry

    lax.fori_loop(0, nodes // 128, turn, 0, unroll=4)

    def pick(i, carry):
        for u in range(unroll):
            t = i * unroll + u
            terms = [tab[pl.ds(idx_ref[k * targets + t], 1), :] for k in range(slots)]
            while len(terms) > 1:
                odd = terms[-1:] if len(terms) % 2 else []
                terms = [a + b for a, b in zip(terms[::2], terms[1::2])] + odd
            rows[pl.ds(t, 1), :] = terms[0]
        return carry

    lax.fori_loop(0, targets // unroll, pick, 0)

    def finish(c, carry):
        at = pl.multiple_of(c * 128, 128)
        mean = rows[pl.ds(at, 128), :].T[0:width, :] / cnt_ref[:, pl.ds(at, 128)].astype(F32)
        both = jnp.concatenate([tx_ref[:, pl.ds(at, 128)].astype(F32), mean], axis=0)
        x_ref[c] = both.astype(BF16)
        xt_ref[c] = both.T.astype(BF16)
        return carry

    lax.fori_loop(0, targets // 128, finish, 0)

    c2 = c2_ref[...]
    node = lax.broadcasted_iota(jnp.int32, (hist_ref.shape[0], c2.shape[1]), 0)
    times = jnp.zeros(node.shape, F32)
    for k in range(n2_ref.shape[0]):
        live = jnp.where(k < c2, n2_ref[k : k + 1, :], -1)
        times = times + jnp.where(node == live, 1.0, 0.0)
    total = dot_rows(hist_ref[...], times.astype(BF16))
    a2_ref[...] = (total / c2.astype(F32)).T.astype(BF16)


def gather_means(tx, frontier, n1, c1, history, n2, c2):
    slots, targets = n1.shape
    live = lax.broadcasted_iota(jnp.int32, n1.shape, 0) < c1[None, :]
    idx = jnp.where(live, n1, frontier.shape[1]).reshape(-1)
    chunks = targets // 128
    deep = 2 * tx.shape[0]
    vmem = pl.BlockSpec(memory_space=pltpu.VMEM)
    return pl.pallas_call(
        functools.partial(gather_kernel, slots, 32),
        out_shape=(
            jax.ShapeDtypeStruct((chunks, deep, 128), BF16),
            jax.ShapeDtypeStruct((chunks, 128, deep), BF16),
            jax.ShapeDtypeStruct((c2.shape[0], history.shape[1]), BF16),
        ),
        in_specs=[pl.BlockSpec(memory_space=pltpu.SMEM)] + [vmem] * 6,
        out_specs=(vmem,) * 3,
        scratch_shapes=[
            pltpu.VMEM((frontier.shape[1] + 8, 128), F32),
            pltpu.VMEM((targets, 128), F32),
        ],
        compiler_params=pltpu.CompilerParams(vmem_limit_bytes=24 << 20),
    )(idx, c1.reshape(1, -1), frontier, tx, history, n2, c2.reshape(1, -1))


class Spread:
    def __init__(self, size, mine, device):
        self.size, self.mine, self.device = size, mine, device

    def peer(self, offset):
        return lax.rem(self.mine + offset, self.size)

    def copies(self, sems, source, target):
        send, recv = sems
        return [
            pltpu.make_async_remote_copy(
                src_ref=source(self.peer(o)),
                dst_ref=target(o),
                send_sem=send.at[o - 1],
                recv_sem=recv.at[o - 1],
                device_id=self.device(self.peer(o)),
                device_id_type=MESH,
            )
            for o in range(1, self.size)
        ]

    def greet(self, barrier):
        for o in range(1, self.size):
            pl.semaphore_signal(
                barrier, inc=1, device_id=self.device(self.peer(o)), device_id_type=MESH
            )


class Total:
    def __init__(self, groups, refs, own, out):
        self.xc, self.y, self.za, self.zb = groups
        (self.rxc, self.vy, self.ry, self.va, self.vb, self.fy, self.fo) = refs[:7]
        sems = refs[7:]
        self.sems = [(sems[2 * i], sems[2 * i + 1]) for i in range(6)]
        self.own, self.out = own, out
        self.live = None
        self.all = []

    def launch(self, copies):
        for copy in copies:
            copy.start()
        self.live = copies
        self.all += copies

    def arrive(self):
        for copy in self.live:
            copy.wait_recv()

    def stage(self, number):
        if number == 0:
            self.launch(self.xc.copies(self.sems[0], lambda p: self.own.at[p], lambda o: self.rxc.at[o - 1]))
            return
        self.arrive()
        if number == 1:
            total = self.own[self.xc.mine]
            for o in range(self.xc.size - 1):
                total = total + self.rxc[o]
            part = self.vy.shape[1]
            for j in range(self.y.size):
                self.vy[j] = total[j * part : (j + 1) * part]
            self.launch(self.y.copies(self.sems[1], lambda p: self.vy.at[p], lambda o: self.ry.at[o - 1]))
        elif number == 2:
            total = self.vy[self.y.mine]
            for o in range(self.y.size - 1):
                total = total + self.ry[o]
            me = self.za.mine
            self.va[me] = total
            self.launch(self.za.copies(self.sems[2], lambda p: self.va.at[me], lambda o: self.va.at[me]))
        elif number == 3:
            total = self.va[0]
            for j in range(1, self.za.size):
                total = total + self.va[j]
            me = self.zb.mine
            self.vb[me] = total
            self.launch(self.zb.copies(self.sems[3], lambda p: self.vb.at[me], lambda o: self.vb.at[me]))
        elif number == 4:
            total = self.vb[0]
            for j in range(1, self.zb.size):
                total = total + self.vb[j]
            me = self.y.mine
            self.fy[me] = total
            self.launch(self.y.copies(self.sems[4], lambda p: self.fy.at[me], lambda o: self.fy.at[me]))
        elif number == 5:
            me = self.xc.mine
            self.launch(self.xc.copies(self.sems[5], lambda p: self.fy, lambda o: self.fo.at[me]))
            self.fo[me] = self.fy[...]
        else:
            part = self.fo.shape[2]
            for q in range(self.xc.size):
                for j in range(self.y.size):
                    at = (q * self.y.size + j) * part
                    self.out[at : at + part, :] = self.fo[q, j]
            for copy in self.all:
                copy.wait_send()


def exchange_kernel(shape, names, *refs):
    nz, ny, nq, zblock = shape
    r = dict(zip(names, refs))
    z = lax.axis_index("feat")
    dp = lax.axis_index("dp")
    q, y = lax.rem(dp, nq), lax.div(dp, nq)
    za, zb = lax.rem(z, zblock), lax.div(z, zblock)
    wrap = lambda v: lax.rem(v + 2 * nz, nz)

    group_q = Spread(nq, q, lambda p: (z, y * nq + p))
    group_y = Spread(ny, y, lambda p: (z, p * nq + q))
    group_a = Spread(zblock, za, lambda p: (zb * zblock + p, dp))
    group_b = Spread(nz // zblock, zb, lambda p: (p * zblock + za, dp))
    groups = (group_q, group_y, group_a, group_b)
    right, left = (wrap(z + 1), dp), (wrap(z - 1), dp)

    barrier = pltpu.get_barrier_semaphore()
    for neighbour in (left, right):
        pl.semaphore_signal(barrier, inc=1, device_id=neighbour, device_id_type=MESH)
    for group in groups:
        group.greet(barrier)

    x, xt, w, og, agg2 = r["x"], r["xt"], r["w"], r["og"], r["agg2"]
    part = r["part"]
    half = xt.shape[1] // 2
    steps_r, steps_l = nz // 2, nz // 2 - 1

    def make_part(j):
        c = wrap(z - steps_l + j)
        part[c] = dot(xt[c], w[...])

    make_part(0)
    make_part(nz - 1)
    out_r, out_l, in_r, in_l = r["out_r"], r["out_l"], r["in_r"], r["in_l"]

    def ring_copy(source, target, sems, s, h, device):
        return pltpu.make_async_remote_copy(
            src_ref=source,
            dst_ref=target.at[s, h],
            send_sem=sems[0].at[s, h],
            recv_sem=sems[1].at[s, h],
            device_id=device,
            device_id_type=MESH,
        )

    sems_r, sems_l = (r["rs_rs"], r["rs_rr"]), (r["rs_ls"], r["rs_lr"])
    rs_r = [[ring_copy(out_r.at[s, h], in_r, sems_r, s, h, right) for h in range(2)] for s in range(steps_r)]
    rs_l = [[ring_copy(out_l.at[s, h], in_l, sems_l, s, h, left) for h in range(2)] for s in range(steps_l)]

    def put(copies, out, arrived, s, h, c):
        value = part[c, h * half : (h + 1) * half, :]
        if s > 0:
            copies[s - 1][h].wait_recv()
            value = value + arrived[s - 1, h].astype(F32)
        out[s, h] = value.astype(BF16)
        copies[s][h].start()

    own_n, own_s = r["own_n"], r["own_s"]
    nparts = own_n.shape[0]
    rows_q = own_n.shape[1]

    def store_own(own, value):
        for j in range(nparts):
            own[j] = value[j * rows_q : (j + 1) * rows_q]

    neigh = Total(groups, [r["n_" + n] for n in TOTAL_NAMES], own_n, r["gn"])
    itself = Total(groups, [r["s_" + n] for n in TOTAL_NAMES], own_s, r["gs"])

    pl.semaphore_wait(barrier, 2 + sum(group.size - 1 for group in groups))

    for h in range(2):
        put(rs_r, out_r, in_r, 0, h, wrap(z + steps_r))
        put(rs_l, out_l, in_l, 0, h, wrap(z - steps_l))

    def rest(j, carry):
        make_part(j)
        return carry

    lax.fori_loop(1, nz - 1, rest, 0)
    store_own(own_n, dot_rows(agg2[...], og[...]))
    neigh.stage(0)
    r["back"][...] = lax.dot_general(
        og[...], r["w2s"][...], (((1,), (1,)), ((), ())), preferred_element_type=F32
    )

    plan_n, plan_s = NEIGH_PLAN[nz], SELF_PLAN[nz]
    for s in range(1, steps_r):
        for h in range(2):
            put(rs_r, out_r, in_r, s, h, wrap(z + steps_r - s))
            if s < steps_l:
                put(rs_l, out_l, in_l, s, h, wrap(z - steps_l + s))
        for number in plan_n.get(s, ()):
            neigh.stage(number)

    ag_r, ag_l, pg, hid = r["ag_r"], r["ag_l"], r["pg"], r["hid"]
    sems_gr, sems_gl = (r["ag_rs"], r["ag_rr"]), (r["ag_ls"], r["ag_lr"])
    fw_r = [[ring_copy(pg.at[h] if s == 0 else ag_r.at[s - 1, h], ag_r, sems_gr, s, h, right) for h in range(2)] for s in range(steps_r)]
    fw_l = [[ring_copy(pg.at[h] if s == 0 else ag_l.at[s - 1, h], ag_l, sems_gl, s, h, left) for h in range(2)] for s in range(steps_l)]

    for h in range(2):
        rs_l[steps_l - 1][h].wait_recv()
        rs_r[steps_r - 1][h].wait_recv()
        span = slice(h * half, (h + 1) * half)
        pre = part[z, span, :] + (in_r[steps_r - 1, h].astype(F32) + in_l[steps_l - 1, h].astype(F32))
        sig = 1.0 / (1.0 + jnp.exp(-pre))
        pg[h] = (r["back"][span, :] * (sig * (1.0 + pre * (1.0 - sig)))).astype(BF16)
        fw_r[0][h].start()
        fw_l[0][h].start()
        hid[span, :] = (pre * sig).astype(BF16)

    store_own(own_s, dot_rows(hid[...], og[...]))
    itself.stage(0)
    r["logits"][...] = (dot(hid[...], r["w2s"][...]) + dot(agg2[...], r["w2n"][...])).astype(BF16)
    for number in plan_n.get("mid", ()):
        neigh.stage(number)

    def term(c, block):
        return dot(x[c], jnp.concatenate([block[0], block[1]], axis=0))

    grad = term(z, pg)
    for s in range(steps_r):
        for h in range(2):
            fw_r[s][h].wait_recv()
            if s + 1 < steps_r:
                fw_r[s + 1][h].start()
            if s < steps_l:
                fw_l[s][h].wait_recv()
                if s + 1 < steps_l:
                    fw_l[s + 1][h].start()
        grad = grad + term(wrap(z - 1 - s), ag_r.at[s])
        if s < steps_l:
            grad = grad + term(wrap(z + 1 + s), ag_l.at[s])
        for number in plan_s.get(s, ()):
            itself.stage(number)

    own_g, rq, gy, go = r["own_g"], r["g_rq"], r["g_y"], r["g_o"]
    rows_g = own_g.shape[1]
    for j in range(nq):
        own_g[j] = grad[j * rows_g : (j + 1) * rows_g]
    first = group_q.copies((r["g_s0"], r["g_r0"]), lambda p: own_g.at[p], lambda o: rq.at[o - 1])
    for copy in first:
        copy.start()
    for number in plan_s.get("a", ()):
        itself.stage(number)
    total = own_g[q]
    for o in range(nq - 1):
        first[o].wait_recv()
        total = total + rq[o]
    gy[y] = total
    second = group_y.copies((r["g_s1"], r["g_r1"]), lambda p: gy.at[y], lambda o: gy.at[y])
    for copy in second:
        copy.start()
    for number in plan_s.get("b", ()):
        itself.stage(number)
    for copy in second:
        copy.wait_recv()
    total = gy[0]
    for j in range(1, ny):
        total = total + gy[j]
    go[q] = total
    third = group_q.copies((r["g_s2"], r["g_r2"]), lambda p: go.at[q], lambda o: go.at[q])
    for copy in third:
        copy.start()
    neigh.stage(6)
    itself.stage(6)
    for copy in third:
        copy.wait_recv()
    for j in range(nq):
        r["g1"][j * rows_g : (j + 1) * rows_g, :] = go[j]
    for copies in rs_r + rs_l + fw_r + fw_l + [first, second, third]:
        for copy in copies:
            copy.wait_send()


TOTAL_NAMES = ("rxc", "vy", "ry", "va", "vb", "fy", "fo") + tuple(
    f"{kind}{i}" for i in range(6) for kind in ("s", "r")
)
NEIGH_PLAN = {16: {3: (1,), 4: (2,), 5: (3,), 6: (4,), 7: (5,)}, 4: {1: (1, 2, 3), "mid": (4, 5)}}
SELF_PLAN = {16: {2: (1,), 3: (2,), 4: (3,), 5: (4,), 6: (5,)}, 4: {0: (1,), 1: (2, 3), "a": (4,), "b": (5,)}}


def exchange(mesh_shape, x, xt, agg2, w, og, w2s, w2n):
    nz, ny, nq, zblock = mesh_shape
    targets, width = og.shape
    half = targets // 2
    rows_q, rows_y, rows_g = width // nq, width // nq // ny, x.shape[1] // nq
    steps_r, steps_l = nz // 2, nz // 2 - 1
    V, D = pltpu.VMEM, pltpu.SemaphoreType.DMA
    scratch = dict(
        part=V((nz, targets, width), F32),
        out_r=V((steps_r, 2, half, width), BF16),
        out_l=V((steps_l, 2, half, width), BF16),
        in_r=V((steps_r, 2, half, width), BF16),
        in_l=V((steps_l, 2, half, width), BF16),
        ag_r=V((steps_r, 2, half, width), BF16),
        ag_l=V((steps_l, 2, half, width), BF16),
        pg=V((2, half, width), BF16),
        hid=V((targets, width), BF16),
        back=V((targets, width), F32),
        own_n=V((nq, rows_q, width), F32),
        own_s=V((nq, rows_q, width), F32),
        own_g=V((nq, rows_g, width), F32),
        g_rq=V((nq - 1, rows_g, width), F32),
        g_y=V((ny, rows_g, width), F32),
        g_o=V((nq, rows_g, width), F32),
    )
    for i, size in enumerate((nq - 1, ny - 1, nq - 1)):
        scratch[f"g_s{i}"] = D((size,))
        scratch[f"g_r{i}"] = D((size,))
    for name in ("rs_r", "rs_l", "ag_r", "ag_l"):
        steps = steps_r if name.endswith("r") else steps_l
        scratch[name + "s"] = D((steps, 2))
        scratch[name + "r"] = D((steps, 2))
    for lead in ("n_", "s_"):
        scratch[lead + "rxc"] = V((nq - 1, rows_q, width), F32)
        scratch[lead + "vy"] = V((ny, rows_y, width), F32)
        scratch[lead + "ry"] = V((ny - 1, rows_y, width), F32)
        scratch[lead + "va"] = V((zblock, rows_y, width), F32)
        scratch[lead + "vb"] = V((nz // zblock, rows_y, width), F32)
        scratch[lead + "fy"] = V((ny, rows_y, width), F32)
        scratch[lead + "fo"] = V((nq, ny, rows_y, width), F32)
        for i, size in enumerate((nq, ny, zblock, nz // zblock, ny, nq)):
            scratch[lead + f"s{i}"] = D((size - 1,))
            scratch[lead + f"r{i}"] = D((size - 1,))
    names = ("x", "xt", "agg2", "w", "og", "w2s", "w2n", "logits", "g1", "gs", "gn") + tuple(scratch)
    vmem = pl.BlockSpec(memory_space=pltpu.VMEM)
    return pl.pallas_call(
        functools.partial(exchange_kernel, mesh_shape, names),
        out_shape=(
            jax.ShapeDtypeStruct((targets, width), BF16),
            jax.ShapeDtypeStruct((x.shape[1], width), F32),
            jax.ShapeDtypeStruct((width, width), F32),
            jax.ShapeDtypeStruct((width, width), F32),
        ),
        in_specs=[vmem] * 7,
        out_specs=(vmem,) * 4,
        scratch_shapes=list(scratch.values()),
        compiler_params=pltpu.CompilerParams(
            collective_id=0, has_side_effects=True, vmem_limit_bytes=32 << 20
        ),
    )(x, xt, agg2, w, og, w2s, w2n)


def hand_out_kernel(logits, g1, gs, gn, o0, o1, o2, o3, o4):
    width = o1.shape[0]
    o0[...] = logits[...]
    o1[...] = g1[0:width, :]
    o2[...] = g1[width:, :]
    o3[...] = gs[...]
    o4[...] = gn[...]


def hand_out(logits, g1, gs, gn):
    vmem = pl.BlockSpec(memory_space=pltpu.VMEM)
    like = lambda a: jax.ShapeDtypeStruct(a.shape, a.dtype)
    piece = jax.ShapeDtypeStruct((g1.shape[0] // 2, g1.shape[1]), F32)
    return pl.pallas_call(
        hand_out_kernel,
        out_shape=(like(logits), piece, piece, like(gs), like(gn)),
        in_specs=[vmem] * 4,
        out_specs=(vmem,) * 5,
        compiler_params=pltpu.CompilerParams(vmem_limit_bytes=8 << 20),
    )(logits, g1, gs, gn)


def local(shape, tx, frontier, n1, c1, w1s, w1n, history, n2, c2, w2s, w2n, og):
    x, xt, agg2 = gather_means(tx, frontier, n1, c1, history, n2, c2)
    w = jnp.concatenate([w1s, w1n], axis=0)
    return hand_out(*exchange(shape, x, xt, agg2, w, og, w2s, w2n))


SPECS = (
    P("feat", "dp"),
    P("feat", "dp"),
    P(None, "dp"),
    P("dp"),
    P("feat", None),
    P("feat", None),
    P(("dp", "feat"), None),
    P(None, ("dp", "feat")),
    P(("dp", "feat")),
    P(),
    P(),
    P(("dp", "feat"), None),
)


def build(mesh, shape):
    return jax.shard_map(
        functools.partial(local, shape),
        mesh=mesh,
        in_specs=SPECS,
        out_specs=(P(("dp", "feat"), None), P("feat", None), P("feat", None), P(), P()),
        check_vma=False,
    )


def solution(mesh):
    return build(mesh, (mesh.shape["feat"], mesh.shape["dp"] // 8, 8, 4))
```

```python
import functools

import jax
import jax.numpy as jnp
from jax import lax
from jax.experimental import pallas as pl
from jax.experimental.pallas import tpu as pltpu
from jax.sharding import PartitionSpec as P

MESH = pl.DeviceIdType.MESH
F32, BF16 = jnp.float32, jnp.bfloat16


def dot(left, right):
    return jnp.dot(left, right, preferred_element_type=F32)


def dot_rows(left, right):
    return lax.dot_general(left, right, (((0,), (0,)), ((), ())), preferred_element_type=F32)


class Spread:
    def __init__(self, size, mine, device):
        self.size, self.mine, self.device = size, mine, device

    def peer(self, offset):
        return lax.rem(self.mine + offset, self.size)

    def copies(self, sems, source, target):
        send, recv = sems
        return [
            pltpu.make_async_remote_copy(
                src_ref=source(self.peer(o)),
                dst_ref=target(o),
                send_sem=send.at[o - 1],
                recv_sem=recv.at[o - 1],
                device_id=self.device(self.peer(o)),
                device_id_type=MESH,
            )
            for o in range(1, self.size)
        ]

    def greet(self, barrier):
        for o in range(1, self.size):
            pl.semaphore_signal(
                barrier, inc=1, device_id=self.device(self.peer(o)), device_id_type=MESH
            )


class Total:
    def __init__(self, groups, refs, own, out):
        self.xc, self.y, self.z = groups
        (self.rxc, self.vy, self.ry, self.vz, self.fy, self.fo) = refs[:6]
        sems = refs[6:]
        self.sems = [(sems[2 * i], sems[2 * i + 1]) for i in range(5)]
        self.own, self.out = own, out

    def copies(self, number):
        sems = self.sems[number]
        if number == 0:
            return self.xc.copies(sems, lambda p: self.own.at[p], lambda o: self.rxc.at[o - 1])
        if number == 1:
            return self.y.copies(sems, lambda p: self.vy.at[p], lambda o: self.ry.at[o - 1])
        if number == 2:
            me = self.z.mine
            return self.z.copies(sems, lambda p: self.vz.at[me], lambda o: self.vz.at[me])
        if number == 3:
            me = self.y.mine
            return self.y.copies(sems, lambda p: self.fy.at[me], lambda o: self.fy.at[me])
        me = self.xc.mine
        return self.xc.copies(sems, lambda p: self.fy, lambda o: self.fo.at[me])

    def stage(self, number):
        if number > 0:
            for copy in self.copies(number - 1):
                copy.wait_recv()
        if number == 1:
            total = self.own[self.xc.mine]
            for o in range(self.xc.size - 1):
                total = total + self.rxc[o]
            part = self.vy.shape[1]
            for j in range(self.y.size):
                self.vy[j] = total[j * part : (j + 1) * part]
        elif number == 2:
            total = self.vy[self.y.mine]
            for o in range(self.y.size - 1):
                total = total + self.ry[o]
            self.vz[self.z.mine] = total
        elif number == 3:
            total = self.vz[0]
            for j in range(1, self.z.size):
                total = total + self.vz[j]
            self.fy[self.y.mine] = total
        elif number == 4:
            self.fo[self.xc.mine] = self.fy[...]
        elif number == 5:
            part = self.fo.shape[2]
            for q in range(self.xc.size):
                for j in range(self.y.size):
                    at = (q * self.y.size + j) * part
                    self.out[at : at + part, :] = self.fo[q, j]
            for done in range(5):
                for copy in self.copies(done):
                    copy.wait_send()
        if number < 5:
            for copy in self.copies(number):
                copy.start()


class Chain:
    def __init__(self, steps, arrived, sems, source, device):
        self.steps, self.arrived, self.sems = steps, arrived, sems
        self.source, self.device = source, device

    def copy(self, s, h):
        return pltpu.make_async_remote_copy(
            src_ref=self.source(s).at[h],
            dst_ref=self.arrived.at[s, h],
            send_sem=self.sems[0].at[s, h],
            recv_sem=self.sems[1].at[s, h],
            device_id=self.device(s),
            device_id_type=MESH,
        )

    def start(self, s, h):
        if s < self.steps:
            self.copy(s, h).start()

    def wait_recv(self, s, h):
        self.copy(s, h).wait_recv()

    def finish(self):
        for s in range(self.steps):
            for h in range(2):
                self.copy(s, h).wait_send()


UNROLL = 16


def step_kernel(shape, names, *refs):
    nz, ny, nq = shape
    r = dict(zip(names, refs))
    z = lax.axis_index("feat")
    dp = lax.axis_index("dp")
    q, y = lax.rem(dp, nq), lax.div(dp, nq)
    wrap = lambda v: lax.rem(v + 2 * nz, nz)

    group_q = Spread(nq, q, lambda p: (z, y * nq + p))
    group_y = Spread(ny, y, lambda p: (z, p * nq + q))
    group_z = Spread(nz, z, lambda p: (p, dp))
    groups = (group_q, group_y, group_z)
    barrier = pltpu.get_barrier_semaphore()
    for group in groups:
        group.greet(barrier)

    x, w, part, og, agg2 = r["x"], r["w"], r["part"], r["og"], r["agg2"]
    f_ref, tab, rows, idx_ref = r["f"], r["tab"], r["rows"], r["idx"]
    width, nodes = f_ref.shape
    targets = r["tx"].shape[1]
    slots = idx_ref.shape[0] // targets
    half = og.shape[0] // 2
    w[0:width, :] = r["w1s"][...]
    w[width:, :] = r["w1n"][...]
    tab[nodes : nodes + 8, :] = jnp.zeros((8, 128), F32)

    def turn(i, carry):
        at = pl.multiple_of(i * 256, 256)
        for j in range(2):
            tab[pl.ds(at + j * 128, 128), 0:width] = f_ref[:, pl.ds(at + j * 128, 128)].astype(F32).T
        return carry

    lax.fori_loop(0, nodes // 256, turn, 0)

    c2 = r["c2"][...]
    node = lax.broadcasted_iota(jnp.int32, (r["hist"].shape[0], c2.shape[1]), 0)
    times = jnp.zeros(node.shape, F32)
    for k in range(r["n2"].shape[0]):
        live = jnp.where(k < c2, r["n2"][k : k + 1, :], -1)
        times = times + jnp.where(node == live, 1.0, 0.0)
    total = dot_rows(r["hist"][...], times.astype(BF16))
    agg2[...] = (total / c2.astype(F32)).T.astype(BF16)

    own_n, own_s = r["own_n"], r["own_s"]
    rows_q = own_n.shape[1]

    def store_own(own, value):
        for j in range(nq):
            own[j] = value[j * rows_q : (j + 1) * rows_q]

    store_own(own_n, dot_rows(agg2[...], og[...]))
    neigh = Total(groups, [r["n_" + n] for n in TOTAL_NAMES], own_n, r["gn"])
    itself = Total(groups, [r["s_" + n] for n in TOTAL_NAMES], own_s, r["gs"])

    def gather(c):
        base = c * 128

        def pick(i, carry):
            for u in range(UNROLL):
                t = base + i * UNROLL + u
                terms = [tab[pl.ds(idx_ref[k * targets + t], 1), :] for k in range(slots)]
                while len(terms) > 1:
                    odd = terms[-1:] if len(terms) % 2 else []
                    terms = [a + b for a, b in zip(terms[::2], terms[1::2])] + odd
                rows[pl.ds(i * UNROLL + u, 1), :] = terms[0]
            return carry

        lax.fori_loop(0, 128 // UNROLL, pick, 0)
        at = pl.multiple_of(base, 128)
        mean = rows[...].T[0:width, :] / r["cnt"][:, pl.ds(at, 128)].astype(F32)
        both = jnp.concatenate([r["tx"][:, pl.ds(at, 128)].astype(F32), mean], axis=0)
        x[c] = both.astype(BF16)
        part[c] = dot(both.T.astype(BF16), w[...])

    jump = nz // 4
    reach_r, reach_l = nz // 2, nz // 2 - 1
    far_r, far_l, near = reach_r - jump + 1, reach_l - jump + 1, jump - 1
    to = lambda offset: (wrap(z + offset), dp)

    def sums(name, steps, sign, far):
        out = r["out_" + name]
        device = lambda s: to(sign * (jump if far and s == steps - 1 else 1))
        return Chain(steps, r["in_" + name], (r["rs_s" + name], r["rs_r" + name]), lambda s: out.at[s], device)

    red_rf, red_lf = sums("rf", far_r, 1, True), sums("lf", far_l, -1, True)
    red_rn, red_ln = sums("rn", near, 1, False), sums("ln", near, -1, False)

    def send_sums(name, chain, s, c):
        for h in range(2):
            value = part[c, h * half : (h + 1) * half, :]
            if s > 0:
                chain.wait_recv(s - 1, h)
                value = value + chain.arrived[s - 1, h].astype(F32)
            r["out_" + name][s, h] = value.astype(BF16)
            chain.start(s, h)

    plan = [("f", 0)]
    for s in range(near):
        plan += [("n", s), ("f", s + 1)]
    plan += [("f", s) for s in range(near + 1, far_r)]
    offsets_r = [reach_r - s if kind == "f" else near - s for kind, s in plan]
    offsets_l = [0 if kind == "f" and s == far_l else (s - reach_l if kind == "f" else s - near) for kind, s in plan]

    def select(i, values):
        chosen = jnp.int32(values[0])
        for j in range(1, len(values)):
            chosen = jnp.where(i == j, values[j], chosen)
        return chosen

    def advance(i, carry):
        gather(wrap(z + select(i, offsets_r)))
        gather(wrap(z + select(i, offsets_l)))
        for j, (kind, s) in enumerate(plan):

            @pl.when(i == j)
            def _():
                if j == 0:
                    pl.semaphore_wait(barrier, sum(group.size - 1 for group in groups))
                if kind == "f":
                    send_sums("rf", red_rf, s, wrap(z + reach_r - s))
                    if s < far_l:
                        send_sums("lf", red_lf, s, wrap(z - reach_l + s))
                else:
                    send_sums("rn", red_rn, s, wrap(z + near - s))
                    send_sums("ln", red_ln, s, wrap(z - near + s))
                for number in NEIGH_PLAN[nz].get(j, ()):
                    neigh.stage(number)

        return carry

    lax.fori_loop(0, len(plan), advance, 0)

    r["back"][...] = lax.dot_general(
        og[...], r["w2s"][...], (((1,), (1,)), ((), ())), preferred_element_type=F32
    )
    later = dot(agg2[...], r["w2n"][...])

    pg, hid = r["pg"], r["hid"]

    def blocks(name, steps, sign, far):
        device = lambda s: to(sign * (jump if far and s == 0 else 1))
        arrived = r["ag_" + name]
        source = lambda s: pg if s == 0 else arrived.at[s - 1]
        return Chain(steps, arrived, (r["ag_s" + name], r["ag_r" + name]), source, device)

    all_rf, all_lf = blocks("rf", far_r, 1, True), blocks("lf", far_l, -1, True)
    all_rn, all_ln = blocks("rn", near, 1, False), blocks("ln", near, -1, False)

    for h in range(2):
        span = slice(h * half, (h + 1) * half)
        pre = part[z, span, :]
        for chain in (red_rf, red_lf, red_rn, red_ln):
            if chain.steps:
                chain.wait_recv(chain.steps - 1, h)
                pre = pre + chain.arrived[chain.steps - 1, h].astype(F32)
        sig = 1.0 / (1.0 + jnp.exp(-pre))
        pg[h] = (r["back"][span, :] * (sig * (1.0 + pre * (1.0 - sig)))).astype(BF16)
        for chain in (all_rf, all_lf, all_rn, all_ln):
            chain.start(0, h)
        hid[span, :] = (pre * sig).astype(BF16)

    store_own(own_s, dot_rows(hid[...], og[...]))
    itself.stage(0)
    r["logits"][...] = (dot(hid[...], r["w2s"][...]) + later).astype(BF16)

    def term(c, block):
        return dot(x[c], jnp.concatenate([block[0], block[1]], axis=0))

    grad = term(z, pg)
    order = [("n", 0)] if near else []
    for s in range(far_r):
        order += [("f", s)] + ([("n", s + 1)] if s + 1 < near else [])
    for j, (kind, s) in enumerate(order):
        pair = ((all_rf, -jump - s), (all_lf, jump + s)) if kind == "f" else ((all_rn, -1 - s), (all_ln, 1 + s))
        pair = [(chain, offset) for chain, offset in pair if s < chain.steps]
        for h in range(2):
            for chain, offset in pair:
                chain.wait_recv(s, h)
                chain.start(s + 1, h)
        for chain, offset in pair:
            grad = grad + term(wrap(z + offset), chain.arrived.at[s])
        for number in AFTER_NEIGH_PLAN[nz].get(j, ()):
            neigh.stage(number)
        for number in SELF_PLAN[nz].get(j, ()):
            itself.stage(number)

    own_g, rq, gy, go = r["own_g"], r["g_rq"], r["g_y"], r["g_o"]
    rows_g = own_g.shape[1]
    for j in range(nq):
        own_g[j] = grad[j * rows_g : (j + 1) * rows_g]
    first = group_q.copies((r["g_s0"], r["g_r0"]), lambda p: own_g.at[p], lambda o: rq.at[o - 1])
    for copy in first:
        copy.start()
    for number in SELF_PLAN[nz].get("a", ()):
        itself.stage(number)
    total = own_g[q]
    for o in range(nq - 1):
        first[o].wait_recv()
        total = total + rq[o]
    gy[y] = total
    second = group_y.copies((r["g_s1"], r["g_r1"]), lambda p: gy.at[y], lambda o: gy.at[y])
    for copy in second:
        copy.start()
    for number in SELF_PLAN[nz].get("b", ()):
        itself.stage(number)
    for chain in (red_rf, red_lf, red_rn, red_ln, all_rf, all_lf, all_rn, all_ln):
        chain.finish()
    neigh.stage(5)
    for copy in second:
        copy.wait_recv()
    total = gy[0]
    for j in range(1, ny):
        total = total + gy[j]
    go[q] = total
    third = group_q.copies((r["g_s2"], r["g_r2"]), lambda p: go.at[q], lambda o: go.at[q])
    for copy in third:
        copy.start()
    for number in SELF_PLAN[nz].get("c", ()):
        itself.stage(number)
    itself.stage(5)
    for copy in third:
        copy.wait_recv()
    for j in range(nq):
        r["g1"][j * rows_g : (j + 1) * rows_g, :] = go[j]
    for copies in (first, second, third):
        for copy in copies:
            copy.wait_send()


TOTAL_NAMES = ("rxc", "vy", "ry", "vz", "fy", "fo") + tuple(
    f"{kind}{i}" for i in range(5) for kind in ("s", "r")
)
NEIGH_PLAN = {16: {0: (0,), 3: (1,), 6: (2,)}, 8: {0: (0,), 2: (1,)}}
AFTER_NEIGH_PLAN = {16: {2: (3,), 5: (4,)}, 8: {0: (2,), 1: (3,), 2: (4,)}}
SELF_PLAN = {
    16: {3: (1,), 6: (2,), "b": (3,), "c": (4,)},
    8: {0: (1,), 1: (2,), "b": (3,), "c": (4,)},
}


def step(shape, idx, cnt, f, tx, hist, n2, c2, w1s, w1n, og, w2s, w2n):
    nz, ny, nq = shape
    targets, width = og.shape
    half = targets // 2
    deep = 2 * tx.shape[0]
    rows_q, rows_y, rows_g = width // nq, width // nq // ny, deep // nq
    jump = nz // 4
    lengths = dict(rf=nz // 2 - jump + 1, lf=nz // 2 - jump, rn=jump - 1, ln=jump - 1)
    V, D = pltpu.VMEM, pltpu.SemaphoreType.DMA
    scratch = dict(
        tab=V((f.shape[1] + 8, 128), F32),
        rows=V((128, 128), F32),
        x=V((nz, deep, 128), BF16),
        w=V((deep, width), BF16),
        agg2=V((targets, width), BF16),
        part=V((nz, targets, width), F32),
        pg=V((2, half, width), BF16),
        hid=V((targets, width), BF16),
        back=V((targets, width), F32),
        own_n=V((nq, rows_q, width), F32),
        own_s=V((nq, rows_q, width), F32),
        own_g=V((nq, rows_g, width), F32),
        g_rq=V((nq - 1, rows_g, width), F32),
        g_y=V((ny, rows_g, width), F32),
        g_o=V((nq, rows_g, width), F32),
    )
    for i, size in enumerate((nq - 1, ny - 1, nq - 1)):
        scratch[f"g_s{i}"] = D((size,))
        scratch[f"g_r{i}"] = D((size,))
    for name, steps in lengths.items():
        for lead in ("out_", "in_", "ag_"):
            scratch[lead + name] = V((steps, 2, half, width), BF16)
        for lead in ("rs_s", "rs_r", "ag_s", "ag_r"):
            scratch[lead + name] = D((steps, 2))
    for lead in ("n_", "s_"):
        scratch[lead + "rxc"] = V((nq - 1, rows_q, width), F32)
        scratch[lead + "vy"] = V((ny, rows_y, width), F32)
        scratch[lead + "ry"] = V((ny - 1, rows_y, width), F32)
        scratch[lead + "vz"] = V((nz, rows_y, width), F32)
        scratch[lead + "fy"] = V((ny, rows_y, width), F32)
        scratch[lead + "fo"] = V((nq, ny, rows_y, width), F32)
        for i, size in enumerate((nq, ny, nz, ny, nq)):
            scratch[lead + f"s{i}"] = D((size - 1,))
            scratch[lead + f"r{i}"] = D((size - 1,))
    inputs = ("idx", "cnt", "f", "tx", "hist", "n2", "c2", "w1s", "w1n", "og", "w2s", "w2n")
    names = inputs + ("logits", "g1", "gs", "gn") + tuple(scratch)
    vmem = pl.BlockSpec(memory_space=pltpu.VMEM)
    return pl.pallas_call(
        functools.partial(step_kernel, shape, names),
        out_shape=(
            jax.ShapeDtypeStruct((targets, width), BF16),
            jax.ShapeDtypeStruct((deep, width), F32),
            jax.ShapeDtypeStruct((width, width), F32),
            jax.ShapeDtypeStruct((width, width), F32),
        ),
        in_specs=[pl.BlockSpec(memory_space=pltpu.SMEM)] + [vmem] * (len(inputs) - 1),
        out_specs=(vmem,) * 4,
        scratch_shapes=list(scratch.values()),
        compiler_params=pltpu.CompilerParams(
            collective_id=0, has_side_effects=True, vmem_limit_bytes=40 << 20
        ),
    )(idx, cnt, f, tx, hist, n2, c2, w1s, w1n, og, w2s, w2n)


def hand_out_kernel(logits, g1, gs, gn, o0, o1, o2, o3, o4):
    width = o1.shape[0]
    o0[...] = logits[...]
    o1[...] = g1[0:width, :]
    o2[...] = g1[width:, :]
    o3[...] = gs[...]
    o4[...] = gn[...]


def hand_out(logits, g1, gs, gn):
    vmem = pl.BlockSpec(memory_space=pltpu.VMEM)
    like = lambda a: jax.ShapeDtypeStruct(a.shape, a.dtype)
    piece = jax.ShapeDtypeStruct((g1.shape[0] // 2, g1.shape[1]), F32)
    return pl.pallas_call(
        hand_out_kernel,
        out_shape=(like(logits), piece, piece, like(gs), like(gn)),
        in_specs=[vmem] * 4,
        out_specs=(vmem,) * 5,
        compiler_params=pltpu.CompilerParams(vmem_limit_bytes=8 << 20),
    )(logits, g1, gs, gn)


def local(shape, tx, frontier, n1, c1, w1s, w1n, history, n2, c2, w2s, w2n, og):
    live = lax.broadcasted_iota(jnp.int32, n1.shape, 0) < c1[None, :]
    idx = jnp.where(live, n1, frontier.shape[1]).reshape(-1)
    return hand_out(
        *step(
            shape, idx, c1.reshape(1, -1), frontier, tx, history, n2, c2.reshape(1, -1),
            w1s, w1n, og, w2s, w2n,
        )
    )


SPECS = (
    P("feat", "dp"),
    P("feat", "dp"),
    P(None, "dp"),
    P("dp"),
    P("feat", None),
    P("feat", None),
    P(("dp", "feat"), None),
    P(None, ("dp", "feat")),
    P(("dp", "feat")),
    P(),
    P(),
    P(("dp", "feat"), None),
)


def build(mesh, shape):
    return jax.shard_map(
        functools.partial(local, shape),
        mesh=mesh,
        in_specs=SPECS,
        out_specs=(P(("dp", "feat"), None), P("feat", None), P("feat", None), P(), P()),
        check_vma=False,
    )


def solution(mesh):
    return build(mesh, (mesh.shape["feat"], mesh.shape["dp"] // 8, 8))
```

```python
import functools

import jax
import jax.numpy as jnp
from jax import lax
from jax.experimental import pallas as pl
from jax.experimental.pallas import tpu as pltpu
from jax.sharding import PartitionSpec as P

MESH = pl.DeviceIdType.MESH
F32, BF16 = jnp.float32, jnp.bfloat16


def dot(left, right):
    return jnp.dot(left, right, preferred_element_type=F32)


def dot_rows(left, right):
    return lax.dot_general(left, right, (((0,), (0,)), ((), ())), preferred_element_type=F32)


class Spread:
    def __init__(self, size, mine, device):
        self.size, self.mine, self.device = size, mine, device

    def peer(self, offset):
        return lax.rem(self.mine + offset, self.size)

    def copies(self, sems, source, target):
        send, recv = sems
        return [
            pltpu.make_async_remote_copy(
                src_ref=source(self.peer(o)),
                dst_ref=target(o),
                send_sem=send.at[o - 1],
                recv_sem=recv.at[o - 1],
                device_id=self.device(self.peer(o)),
                device_id_type=MESH,
            )
            for o in range(1, self.size)
        ]

    def greet(self, barrier):
        for o in range(1, self.size):
            pl.semaphore_signal(
                barrier, inc=1, device_id=self.device(self.peer(o)), device_id_type=MESH
            )


class Total:
    def __init__(self, groups, refs, own, out):
        self.xc, self.y, self.z = groups
        (self.rxc, self.vy, self.ry, self.vz, self.fy, self.fo) = refs[:6]
        sems = refs[6:]
        self.sems = [(sems[2 * i], sems[2 * i + 1]) for i in range(5)]
        self.own, self.out = own, out

    def copies(self, number):
        sems = self.sems[number]
        if number == 0:
            return self.xc.copies(sems, lambda p: self.own.at[p], lambda o: self.rxc.at[o - 1])
        if number == 1:
            return self.y.copies(sems, lambda p: self.vy.at[p], lambda o: self.ry.at[o - 1])
        if number == 2:
            me = self.z.mine
            return self.z.copies(sems, lambda p: self.vz.at[me], lambda o: self.vz.at[me])
        if number == 3:
            me = self.y.mine
            return self.y.copies(sems, lambda p: self.fy.at[me], lambda o: self.fy.at[me])
        me = self.xc.mine
        return self.xc.copies(sems, lambda p: self.fy, lambda o: self.fo.at[me])

    def stage(self, number):
        if number > 0:
            for copy in self.copies(number - 1):
                copy.wait_recv()
        if number == 1:
            total = self.own[self.xc.mine]
            for o in range(self.xc.size - 1):
                total = total + self.rxc[o]
            part = self.vy.shape[1]
            for j in range(self.y.size):
                self.vy[j] = total[j * part : (j + 1) * part]
        elif number == 2:
            total = self.vy[self.y.mine]
            for o in range(self.y.size - 1):
                total = total + self.ry[o]
            self.vz[self.z.mine] = total
        elif number == 3:
            total = self.vz[0]
            for j in range(1, self.z.size):
                total = total + self.vz[j]
            self.fy[self.y.mine] = total
        elif number == 4:
            self.fo[self.xc.mine] = self.fy[...]
        elif number == 5:
            part = self.fo.shape[2]
            for q in range(self.xc.size):
                for j in range(self.y.size):
                    at = (q * self.y.size + j) * part
                    self.out[at : at + part, :] = self.fo[q, j]
            for done in range(5):
                for copy in self.copies(done):
                    copy.wait_send()
        if number < 5:
            for copy in self.copies(number):
                copy.start()


class Chain:
    def __init__(self, steps, arrived, sems, source, device):
        self.steps, self.arrived, self.sems = steps, arrived, sems
        self.source, self.device = source, device

    def copy(self, s, h):
        return pltpu.make_async_remote_copy(
            src_ref=self.source(s).at[h],
            dst_ref=self.arrived.at[s, h],
            send_sem=self.sems[0].at[s, h],
            recv_sem=self.sems[1].at[s, h],
            device_id=self.device(s),
            device_id_type=MESH,
        )

    def start(self, s, h):
        if s < self.steps:
            self.copy(s, h).start()

    def wait_recv(self, s, h):
        self.copy(s, h).wait_recv()

    def finish(self):
        for s in range(self.steps):
            for h in range(2):
                self.copy(s, h).wait_send()


UNROLL = 16


def step_kernel(shape, names, *refs):
    nz, ny, nq = shape
    r = dict(zip(names, refs))
    loads = {
        name: pltpu.make_async_copy(r[name], r["v_" + name], r["in_sem"].at[i])
        for i, name in enumerate(INPUTS)
    }
    for load in loads.values():
        load.start()

    def take(*wanted):
        for name in wanted:
            loads[name].wait()

    z = lax.axis_index("feat")
    dp = lax.axis_index("dp")
    q, y = lax.rem(dp, nq), lax.div(dp, nq)
    wrap = lambda v: lax.rem(v + 2 * nz, nz)

    group_q = Spread(nq, q, lambda p: (z, y * nq + p))
    group_y = Spread(ny, y, lambda p: (z, p * nq + q))
    group_z = Spread(nz, z, lambda p: (p, dp))
    groups = (group_q, group_y, group_z)
    barrier = pltpu.get_barrier_semaphore()
    for group in groups:
        group.greet(barrier)

    r = {**r, **{name: r["v_" + name] for name in INPUTS}}
    x, w, part, og, agg2 = r["x"], r["w"], r["part"], r["og"], r["agg2"]
    f_ref, tab, rows, idx_ref = r["f"], r["tab"], r["rows"], r["idx"]
    width, nodes = f_ref.shape
    targets = r["tx"].shape[1]
    take("f")
    slots = idx_ref.shape[0] // targets
    half = og.shape[1] // 2
    tab[nodes : nodes + 8, :] = jnp.zeros((8, 128), F32)

    def turn(i, carry):
        at = pl.multiple_of(i * 256, 256)
        for j in range(2):
            tab[pl.ds(at + j * 128, 128), 0:width] = f_ref[:, pl.ds(at + j * 128, 128)].astype(F32).T
        return carry

    lax.fori_loop(0, nodes // 256, turn, 0)

    take("w1s", "w1n", "idx", "cnt", "tx")
    w[:, 0:width] = r["w1s"][...].astype(F32).T.astype(BF16)
    w[:, width:] = r["w1n"][...].astype(F32).T.astype(BF16)

    own_n, own_s = r["own_n"], r["own_s"]
    rows_q = own_n.shape[1]

    def store_own(own, value):
        for j in range(nq):
            own[j] = value[j * rows_q : (j + 1) * rows_q]

    neigh = Total(groups, [r["n_" + n] for n in TOTAL_NAMES], own_n, r["gn"])
    itself = Total(groups, [r["s_" + n] for n in TOTAL_NAMES], own_s, r["gs"])

    def gather(chunks):
        for place, c in enumerate(chunks):
            base = c * 128

            def pick(i, carry):
                for u in range(UNROLL):
                    t = base + i * UNROLL + u
                    terms = [tab[pl.ds(idx_ref[k * targets + t], 1), :] for k in range(slots)]
                    while len(terms) > 1:
                        odd = terms[-1:] if len(terms) % 2 else []
                        terms = [a + b for a, b in zip(terms[::2], terms[1::2])] + odd
                    rows[place, pl.ds(i * UNROLL + u, 1), :] = terms[0]
                return carry

            lax.fori_loop(0, 128 // UNROLL, pick, 0)
        for place, c in enumerate(chunks):
            at = pl.multiple_of(c * 128, 128)
            mean = rows[place].T[0:width, :] / r["cnt"][:, pl.ds(at, 128)].astype(F32)
            x[c, 0:width] = r["tx"][:, pl.ds(at, 128)]
            x[c, width:] = mean.astype(BF16)
        for c in chunks:
            part[c] = dot(w[...], x[c])

    jump = nz // 4
    reach_r, reach_l = nz // 2, nz // 2 - 1
    far_r, far_l, near = reach_r - jump + 1, reach_l - jump + 1, jump - 1
    to = lambda offset: (wrap(z + offset), dp)

    def sums(name, steps, sign, far):
        out = r["out_" + name]
        device = lambda s: to(sign * (jump if far and s == steps - 1 else 1))
        return Chain(steps, r["in_" + name], (r["rs_s" + name], r["rs_r" + name]), lambda s: out.at[s], device)

    red_rf, red_lf = sums("rf", far_r, 1, True), sums("lf", far_l, -1, True)
    red_rn, red_ln = sums("rn", near, 1, False), sums("ln", near, -1, False)

    def send_sums(name, chain, s, c):
        for h in range(2):
            value = part[c, h * half : (h + 1) * half, :]
            if s > 0:
                chain.wait_recv(s - 1, h)
                value = value + chain.arrived[s - 1, h].astype(F32)
            r["out_" + name][s, h] = value.astype(BF16)
            chain.start(s, h)

    plan = [("f", 0)]
    for s in range(near):
        plan += [("n", s), ("f", s + 1)]
    plan += [("f", s) for s in range(near + 1, far_r)]
    offsets_r = [reach_r - s if kind == "f" else near - s for kind, s in plan]
    offsets_l = [0 if kind == "f" and s == far_l else (s - reach_l if kind == "f" else s - near) for kind, s in plan]

    def select(i, values):
        chosen = jnp.int32(values[0])
        for j in range(1, len(values)):
            chosen = jnp.where(i == j, values[j], chosen)
        return chosen

    def advance(i, carry):
        gather([wrap(z + select(i, offsets_r)), wrap(z + select(i, offsets_l))])
        for j, (kind, s) in enumerate(plan):

            @pl.when(i == j)
            def _():
                if j == 0:
                    pl.semaphore_wait(barrier, sum(group.size - 1 for group in groups))
                if kind == "f":
                    send_sums("rf", red_rf, s, wrap(z + reach_r - s))
                    if s < far_l:
                        send_sums("lf", red_lf, s, wrap(z - reach_l + s))
                else:
                    send_sums("rn", red_rn, s, wrap(z + near - s))
                    send_sums("ln", red_ln, s, wrap(z - near + s))
        return carry

    lax.fori_loop(0, len(plan), advance, 0)

    take("hist", "n2", "c2", "og", "w2s", "w2n")
    c2 = r["c2"][...]
    node = lax.broadcasted_iota(jnp.int32, (r["hist"].shape[0], c2.shape[1]), 0)
    times = jnp.zeros(node.shape, F32)
    for k in range(r["n2"].shape[0]):
        live = jnp.where(k < c2, r["n2"][k : k + 1, :], -1)
        times = times + jnp.where(node == live, 1.0, 0.0)
    total = dot_rows(r["hist"][...], times.astype(BF16))
    agg2[...] = (total / c2.astype(F32)).astype(BF16)

    store_own(own_n, dot(agg2[...], og[...]))
    neigh.stage(0)
    r["back"][...] = lax.dot_general(
        r["w2s"][...], og[...], (((1,), (1,)), ((), ())), preferred_element_type=F32
    )
    later = dot_rows(agg2[...], r["w2n"][...])

    pg, hid = r["pg"], r["hid"]

    def blocks(name, steps, sign, far):
        device = lambda s: to(sign * (jump if far and s == 0 else 1))
        arrived = r["ag_" + name]
        source = lambda s: pg if s == 0 else arrived.at[s - 1]
        return Chain(steps, arrived, (r["ag_s" + name], r["ag_r" + name]), source, device)

    all_rf, all_lf = blocks("rf", far_r, 1, True), blocks("lf", far_l, -1, True)
    all_rn, all_ln = blocks("rn", near, 1, False), blocks("ln", near, -1, False)

    for h in range(2):
        span = slice(h * half, (h + 1) * half)
        pre = part[z, span, :]
        for chain in (red_rf, red_lf, red_rn, red_ln):
            if chain.steps:
                chain.wait_recv(chain.steps - 1, h)
                pre = pre + chain.arrived[chain.steps - 1, h].astype(F32)
        sig = 1.0 / (1.0 + jnp.exp(-pre))
        pg[h] = (r["back"][span, :] * (sig * (1.0 + pre * (1.0 - sig)))).astype(BF16)
        for chain in (all_rf, all_lf, all_rn, all_ln):
            chain.start(0, h)
        hid[span, :] = (pre * sig).astype(BF16)

    store_own(own_s, dot(hid[...], og[...]))
    itself.stage(0)
    r["logits"][...] = (dot_rows(hid[...], r["w2s"][...]) + later).astype(BF16)

    def term(c, block):
        whole = jnp.concatenate([block[0], block[1]], axis=0)
        return lax.dot_general(x[c], whole, (((1,), (1,)), ((), ())), preferred_element_type=F32)

    def sums_on(point):
        for which, number in PLAN[nz].get(point, ()):
            (neigh if which == "n" else itself).stage(number)

    grad = term(z, pg)
    order = [("n", 0)] if near else []
    for s in range(far_r):
        order += [("f", s)] + ([("n", s + 1)] if s + 1 < near else [])
    for j, (kind, s) in enumerate(order):
        pair = ((all_rf, -jump - s), (all_lf, jump + s)) if kind == "f" else ((all_rn, -1 - s), (all_ln, 1 + s))
        pair = [(chain, offset) for chain, offset in pair if s < chain.steps]
        for h in range(2):
            for chain, offset in pair:
                chain.wait_recv(s, h)
                chain.start(s + 1, h)
        for chain, offset in pair:
            grad = grad + term(wrap(z + offset), chain.arrived.at[s])
        sums_on(j)

    own_g, rq, gy, go = r["own_g"], r["g_rq"], r["g_y"], r["g_o"]
    rows_g = own_g.shape[1]
    for j in range(nq):
        own_g[j] = grad[j * rows_g : (j + 1) * rows_g].astype(BF16)
    first = group_q.copies((r["g_s0"], r["g_r0"]), lambda p: own_g.at[p], lambda o: rq.at[o - 1])
    for copy in first:
        copy.start()
    sums_on("a")
    total = own_g[q].astype(F32)
    for o in range(nq - 1):
        first[o].wait_recv()
        total = total + rq[o].astype(F32)
    gy[y] = total.astype(BF16)
    second = group_y.copies((r["g_s1"], r["g_r1"]), lambda p: gy.at[y], lambda o: gy.at[y])
    for copy in second:
        copy.start()
    sums_on("b")
    for chain in (red_rf, red_lf, red_rn, red_ln, all_rf, all_lf, all_rn, all_ln):
        chain.finish()
    neigh.stage(5)
    for copy in second:
        copy.wait_recv()
    total = gy[0].astype(F32)
    for j in range(1, ny):
        total = total + gy[j].astype(F32)
    go[q] = total
    third = group_q.copies((r["g_s2"], r["g_r2"]), lambda p: go.at[q], lambda o: go.at[q])
    for copy in third:
        copy.start()
    sums_on("c")
    itself.stage(5)
    for copy in third:
        copy.wait_recv()
    for j in range(nq):
        r["g1"][j * rows_g : (j + 1) * rows_g, :] = go[j]
    for copies in (first, second, third):
        for copy in copies:
            copy.wait_send()


TOTAL_NAMES = ("rxc", "vy", "ry", "vz", "fy", "fo") + tuple(
    f"{kind}{i}" for i in range(5) for kind in ("s", "r")
)
PLAN = {
    16: {2: ("n1",), 3: ("s1",), 4: ("n2",), 5: ("s2",), "a": ("n3", "s3"), "b": ("n4", "s4")},
    8: {0: ("n1", "s1"), 1: ("n2", "s2"), "a": ("n3", "s3"), "b": ("n4", "s4")},
}
PLAN = {
    size: {point: tuple((stage[0], int(stage[1])) for stage in stages) for point, stages in plan.items()}
    for size, plan in PLAN.items()
}
INPUTS = ("f", "idx", "cnt", "tx", "w1s", "w1n", "hist", "n2", "c2", "og", "w2s", "w2n")


def step(shape, idx, cnt, f, tx, hist, n2, c2, w1s, w1n, og, w2s, w2n):
    nz, ny, nq = shape
    targets, width = og.shape
    half = width // 2
    deep = 2 * tx.shape[0]
    rows_q, rows_y, rows_g = width // nq, width // nq // ny, deep // nq
    jump = nz // 4
    lengths = dict(rf=nz // 2 - jump + 1, lf=nz // 2 - jump, rn=jump - 1, ln=jump - 1)
    V, D = pltpu.VMEM, pltpu.SemaphoreType.DMA
    scratch = dict(
        tab=V((f.shape[1] + 8, 128), F32),
        rows=V((2, 128, 128), F32),
        x=V((nz, deep, 128), BF16),
        w=V((width, deep), BF16),
        agg2=V((width, targets), BF16),
        part=V((nz, width, targets), F32),
        pg=V((2, half, targets), BF16),
        hid=V((width, targets), BF16),
        back=V((width, targets), F32),
        own_n=V((nq, rows_q, width), F32),
        own_s=V((nq, rows_q, width), F32),
        own_g=V((nq, rows_g, width), BF16),
        g_rq=V((nq - 1, rows_g, width), BF16),
        g_y=V((ny, rows_g, width), BF16),
        g_o=V((nq, rows_g, width), F32),
    )
    for i, size in enumerate((nq - 1, ny - 1, nq - 1)):
        scratch[f"g_s{i}"] = D((size,))
        scratch[f"g_r{i}"] = D((size,))
    for name, steps in lengths.items():
        for lead in ("out_", "in_", "ag_"):
            scratch[lead + name] = V((steps, 2, half, targets), BF16)
        for lead in ("rs_s", "rs_r", "ag_s", "ag_r"):
            scratch[lead + name] = D((steps, 2))
    for lead in ("n_", "s_"):
        scratch[lead + "rxc"] = V((nq - 1, rows_q, width), F32)
        scratch[lead + "vy"] = V((ny, rows_y, width), F32)
        scratch[lead + "ry"] = V((ny - 1, rows_y, width), F32)
        scratch[lead + "vz"] = V((nz, rows_y, width), F32)
        scratch[lead + "fy"] = V((ny, rows_y, width), F32)
        scratch[lead + "fo"] = V((nq, ny, rows_y, width), F32)
        for i, size in enumerate((nq, ny, nz, ny, nq)):
            scratch[lead + f"s{i}"] = D((size - 1,))
            scratch[lead + f"r{i}"] = D((size - 1,))
    given = dict(f=f, idx=idx, cnt=cnt, tx=tx, w1s=w1s, w1n=w1n, hist=hist, n2=n2, c2=c2, og=og, w2s=w2s, w2n=w2n)
    for name in INPUTS:
        place = pltpu.SMEM if name == "idx" else V
        scratch["v_" + name] = place(given[name].shape, given[name].dtype)
    scratch["in_sem"] = D((len(INPUTS),))
    names = INPUTS + ("logits", "g1", "gs", "gn") + tuple(scratch)
    vmem = pl.BlockSpec(memory_space=pltpu.VMEM)
    return pl.pallas_call(
        functools.partial(step_kernel, shape, names),
        out_shape=(
            jax.ShapeDtypeStruct((targets, width), BF16),
            jax.ShapeDtypeStruct((deep, width), F32),
            jax.ShapeDtypeStruct((width, width), F32),
            jax.ShapeDtypeStruct((width, width), F32),
        ),
        in_specs=[pl.BlockSpec(memory_space=pl.ANY)] * len(INPUTS),
        out_specs=(vmem,) * 4,
        scratch_shapes=list(scratch.values()),
        compiler_params=pltpu.CompilerParams(
            collective_id=0, has_side_effects=True, vmem_limit_bytes=56 << 20
        ),
    )(*[given[name] for name in INPUTS])


def hand_out_kernel(logits, g1, gs, gn, o0, o1, o2, o3, o4):
    width = o1.shape[0]
    o0[...] = logits[...]
    o1[...] = g1[0:width, :]
    o2[...] = g1[width:, :]
    o3[...] = gs[...]
    o4[...] = gn[...]


def hand_out(logits, g1, gs, gn):
    vmem = pl.BlockSpec(memory_space=pltpu.VMEM)
    like = lambda a: jax.ShapeDtypeStruct(a.shape, a.dtype)
    piece = jax.ShapeDtypeStruct((g1.shape[0] // 2, g1.shape[1]), F32)
    return pl.pallas_call(
        hand_out_kernel,
        out_shape=(like(logits), piece, piece, like(gs), like(gn)),
        in_specs=[vmem] * 4,
        out_specs=(vmem,) * 5,
        compiler_params=pltpu.CompilerParams(vmem_limit_bytes=8 << 20),
    )(logits, g1, gs, gn)


def local(shape, tx, frontier, n1, c1, w1s, w1n, history, n2, c2, w2s, w2n, og):
    live = lax.broadcasted_iota(jnp.int32, n1.shape, 0) < c1[None, :]
    idx = jnp.where(live, n1, frontier.shape[1]).reshape(-1)
    return hand_out(
        *step(
            shape, idx, c1.reshape(1, -1), frontier, tx, history, n2, c2.reshape(1, -1),
            w1s, w1n, og, w2s, w2n,
        )
    )


SPECS = (
    P("feat", "dp"),
    P("feat", "dp"),
    P(None, "dp"),
    P("dp"),
    P("feat", None),
    P("feat", None),
    P(("dp", "feat"), None),
    P(None, ("dp", "feat")),
    P(("dp", "feat")),
    P(),
    P(),
    P(("dp", "feat"), None),
)


def build(mesh, shape):
    return jax.shard_map(
        functools.partial(local, shape),
        mesh=mesh,
        in_specs=SPECS,
        out_specs=(P(("dp", "feat"), None), P("feat", None), P("feat", None), P(), P()),
        check_vma=False,
    )


def solution(mesh):
    return build(mesh, (mesh.shape["feat"], mesh.shape["dp"] // 8, 8))
```

```python
import functools

import jax
import jax.numpy as jnp
from jax import lax
from jax.experimental import pallas as pl
from jax.experimental.pallas import tpu as pltpu
from jax.sharding import PartitionSpec as P

MESH = pl.DeviceIdType.MESH
F32, BF16 = jnp.float32, jnp.bfloat16


def dot(left, right):
    return jnp.dot(left, right, preferred_element_type=F32)


def dot_rows(left, right):
    return lax.dot_general(left, right, (((0,), (0,)), ((), ())), preferred_element_type=F32)


class Spread:
    def __init__(self, size, mine, device):
        self.size, self.mine, self.device = size, mine, device

    def peer(self, offset):
        return lax.rem(self.mine + offset, self.size)

    def copies(self, sems, source, target):
        send, recv = sems
        return [
            pltpu.make_async_remote_copy(
                src_ref=source(self.peer(o)),
                dst_ref=target(o),
                send_sem=send.at[o - 1],
                recv_sem=recv.at[o - 1],
                device_id=self.device(self.peer(o)),
                device_id_type=MESH,
            )
            for o in range(1, self.size)
        ]

    def greet(self, barrier):
        for o in range(1, self.size):
            pl.semaphore_signal(
                barrier, inc=1, device_id=self.device(self.peer(o)), device_id_type=MESH
            )


class Total:
    def __init__(self, groups, refs, own, out):
        self.xc, self.y, self.z = groups
        (self.rxc, self.vy, self.ry, self.vz, self.fy, self.fo) = refs[:6]
        sems = refs[6:]
        self.sems = [(sems[2 * i], sems[2 * i + 1]) for i in range(5)]
        self.own, self.out = own, out

    def copies(self, number):
        sems = self.sems[number]
        if number == 0:
            return self.xc.copies(sems, lambda p: self.own.at[p], lambda o: self.rxc.at[o - 1])
        if number == 1:
            return self.y.copies(sems, lambda p: self.vy.at[p], lambda o: self.ry.at[o - 1])
        if number == 2:
            me = self.z.mine
            return self.z.copies(sems, lambda p: self.vz.at[me], lambda o: self.vz.at[me])
        if number == 3:
            me = self.y.mine
            return self.y.copies(sems, lambda p: self.fy.at[me], lambda o: self.fy.at[me])
        me = self.xc.mine
        return self.xc.copies(sems, lambda p: self.fy, lambda o: self.fo.at[me])

    def stage(self, number):
        if number > 0:
            for copy in self.copies(number - 1):
                copy.wait_recv()
        if number == 1:
            total = self.own[self.xc.mine]
            for o in range(self.xc.size - 1):
                total = total + self.rxc[o]
            part = self.vy.shape[1]
            for j in range(self.y.size):
                self.vy[j] = total[j * part : (j + 1) * part]
        elif number == 2:
            total = self.vy[self.y.mine]
            for o in range(self.y.size - 1):
                total = total + self.ry[o]
            self.vz[self.z.mine] = total
        elif number == 3:
            total = self.vz[0]
            for j in range(1, self.z.size):
                total = total + self.vz[j]
            self.fy[self.y.mine] = total
        elif number == 4:
            self.fo[self.xc.mine] = self.fy[...]
        elif number == 5:
            part = self.fo.shape[2]
            for q in range(self.xc.size):
                for j in range(self.y.size):
                    at = (q * self.y.size + j) * part
                    self.out[at : at + part, :] = self.fo[q, j]
            for done in range(5):
                for copy in self.copies(done):
                    copy.wait_send()
        if number < 5:
            for copy in self.copies(number):
                copy.start()


class Chain:
    def __init__(self, steps, arrived, sems, source, device):
        self.steps, self.arrived, self.sems = steps, arrived, sems
        self.source, self.device = source, device

    def copy(self, s, h):
        return pltpu.make_async_remote_copy(
            src_ref=self.source(s).at[h],
            dst_ref=self.arrived.at[s, h],
            send_sem=self.sems[0].at[s, h],
            recv_sem=self.sems[1].at[s, h],
            device_id=self.device(s),
            device_id_type=MESH,
        )

    def start(self, s, h):
        if s < self.steps:
            self.copy(s, h).start()

    def wait_recv(self, s, h):
        self.copy(s, h).wait_recv()

    def finish(self):
        for s in range(self.steps):
            for h in range(2):
                self.copy(s, h).wait_send()


UNROLL = 32


def step_kernel(shape, names, *refs):
    nz, ny, nq = shape
    r = dict(zip(names, refs))
    loads = {
        name: pltpu.make_async_copy(r[name], r["v_" + name], r["in_sem"].at[i])
        for i, name in enumerate(INPUTS)
    }
    for load in loads.values():
        load.start()

    def take(*wanted):
        for name in wanted:
            loads[name].wait()

    z = lax.axis_index("feat")
    dp = lax.axis_index("dp")
    q, y = lax.rem(dp, nq), lax.div(dp, nq)
    wrap = lambda v: lax.rem(v + 2 * nz, nz)

    group_q = Spread(nq, q, lambda p: (z, y * nq + p))
    group_y = Spread(ny, y, lambda p: (z, p * nq + q))
    group_z = Spread(nz, z, lambda p: (p, dp))
    groups = (group_q, group_y, group_z)
    barrier = pltpu.get_barrier_semaphore()
    for group in groups:
        group.greet(barrier)

    r = {**r, **{name: r["v_" + name] for name in INPUTS}}
    x, w, part, og, agg2 = r["x"], r["w"], r["part"], r["og"], r["agg2"]
    f_ref, tab, rows, idx_ref = r["f"], r["tab"], r["rows"], r["idx"]
    width, nodes = f_ref.shape
    targets = r["tx"].shape[1]
    take("f")
    slots = idx_ref.shape[0] // targets
    half = og.shape[1] // 2
    tab[nodes : nodes + 8, :] = jnp.zeros((8, 128), F32)

    def turn(i, carry):
        at = pl.multiple_of(i * 256, 256)
        for j in range(2):
            tab[pl.ds(at + j * 128, 128), 0:width] = f_ref[:, pl.ds(at + j * 128, 128)].astype(F32).T
        return carry

    lax.fori_loop(0, nodes // 256, turn, 0)

    take("w1s", "w1n", "idx", "cnt", "tx")
    w[:, 0:width] = r["w1s"][...].astype(F32).T.astype(BF16)
    w[:, width:] = r["w1n"][...].astype(F32).T.astype(BF16)

    own_n, own_s = r["own_n"], r["own_s"]
    rows_q = own_n.shape[1]

    def store_own(own, value):
        for j in range(nq):
            own[j] = value[j * rows_q : (j + 1) * rows_q]

    neigh = Total(groups, [r["n_" + n] for n in TOTAL_NAMES], own_n, r["gn"])
    itself = Total(groups, [r["s_" + n] for n in TOTAL_NAMES], own_s, r["gs"])

    def gather(chunks):
        for place, c in enumerate(chunks):
            base = c * 128

            def pick(i, carry):
                for u in range(UNROLL):
                    t = base + i * UNROLL + u
                    terms = [tab[pl.ds(idx_ref[k * targets + t], 1), :] for k in range(slots)]
                    while len(terms) > 1:
                        odd = terms[-1:] if len(terms) % 2 else []
                        terms = [a + b for a, b in zip(terms[::2], terms[1::2])] + odd
                    rows[place, pl.ds(i * UNROLL + u, 1), :] = terms[0]
                return carry

            lax.fori_loop(0, 128 // UNROLL, pick, 0)
        for place, c in enumerate(chunks):
            at = pl.multiple_of(c * 128, 128)
            mean = rows[place].T[0:width, :] / r["cnt"][:, pl.ds(at, 128)].astype(F32)
            x[c, 0:width] = r["tx"][:, pl.ds(at, 128)]
            x[c, width:] = mean.astype(BF16)
        for c in chunks:
            part[c] = dot(w[...], x[c])

    jump = nz // 4
    reach_r, reach_l = nz // 2, nz // 2 - 1
    far_r, far_l, near = reach_r - jump + 1, reach_l - jump + 1, jump - 1
    to = lambda offset: (wrap(z + offset), dp)

    def sums(name, steps, sign, far):
        out = r["out_" + name]
        device = lambda s: to(sign * (jump if far and s == steps - 1 else 1))
        return Chain(steps, r["in_" + name], (r["rs_s" + name], r["rs_r" + name]), lambda s: out.at[s], device)

    red_rf, red_lf = sums("rf", far_r, 1, True), sums("lf", far_l, -1, True)
    red_rn, red_ln = sums("rn", near, 1, False), sums("ln", near, -1, False)

    def send_sums(name, chain, s, c):
        for h in range(2):
            value = part[c, h * half : (h + 1) * half, :]
            if s > 0:
                chain.wait_recv(s - 1, h)
                value = value + chain.arrived[s - 1, h].astype(F32)
            r["out_" + name][s, h] = value.astype(BF16)
            chain.start(s, h)

    plan = [("f", 0)]
    for s in range(near):
        plan += [("n", s), ("f", s + 1)]
    plan += [("f", s) for s in range(near + 1, far_r)]
    offsets_r = [reach_r - s if kind == "f" else near - s for kind, s in plan]
    offsets_l = [0 if kind == "f" and s == far_l else (s - reach_l if kind == "f" else s - near) for kind, s in plan]

    def select(i, values):
        chosen = jnp.int32(values[0])
        for j in range(1, len(values)):
            chosen = jnp.where(i == j, values[j], chosen)
        return chosen

    def advance(i, carry):
        gather([wrap(z + select(i, offsets_r)), wrap(z + select(i, offsets_l))])
        for j, (kind, s) in enumerate(plan):

            @pl.when(i == j)
            def _():
                if j == 0:
                    pl.semaphore_wait(barrier, sum(group.size - 1 for group in groups))
                if kind == "f":
                    send_sums("rf", red_rf, s, wrap(z + reach_r - s))
                    if s < far_l:
                        send_sums("lf", red_lf, s, wrap(z - reach_l + s))
                else:
                    send_sums("rn", red_rn, s, wrap(z + near - s))
                    send_sums("ln", red_ln, s, wrap(z - near + s))
        return carry

    lax.fori_loop(0, len(plan), advance, 0)

    take("hist", "n2", "c2", "og", "w2s", "w2n")
    c2 = r["c2"][...]
    node = lax.broadcasted_iota(jnp.int32, (r["hist"].shape[0], c2.shape[1]), 0)
    times = jnp.zeros(node.shape, F32)
    for k in range(r["n2"].shape[0]):
        live = jnp.where(k < c2, r["n2"][k : k + 1, :], -1)
        times = times + jnp.where(node == live, 1.0, 0.0)
    total = dot_rows(r["hist"][...], times.astype(BF16))
    agg2[...] = (total / c2.astype(F32)).astype(BF16)

    store_own(own_n, dot(agg2[...], og[...]))
    neigh.stage(0)
    r["back"][...] = lax.dot_general(
        r["w2s"][...], og[...], (((1,), (1,)), ((), ())), preferred_element_type=F32
    )
    later = dot_rows(agg2[...], r["w2n"][...])

    pg, hid = r["pg"], r["hid"]

    def blocks(name, steps, sign, far):
        device = lambda s: to(sign * (jump if far and s == 0 else 1))
        arrived = r["ag_" + name]
        source = lambda s: pg if s == 0 else arrived.at[s - 1]
        return Chain(steps, arrived, (r["ag_s" + name], r["ag_r" + name]), source, device)

    all_rf, all_lf = blocks("rf", far_r, 1, True), blocks("lf", far_l, -1, True)
    all_rn, all_ln = blocks("rn", near, 1, False), blocks("ln", near, -1, False)

    for h in range(2):
        span = slice(h * half, (h + 1) * half)
        pre = part[z, span, :]
        for chain in (red_rf, red_lf, red_rn, red_ln):
            if chain.steps:
                chain.wait_recv(chain.steps - 1, h)
                pre = pre + chain.arrived[chain.steps - 1, h].astype(F32)
        sig = 1.0 / (1.0 + jnp.exp(-pre))
        pg[h] = (r["back"][span, :] * (sig * (1.0 + pre * (1.0 - sig)))).astype(BF16)
        for chain in (all_rf, all_lf, all_rn, all_ln):
            chain.start(0, h)
        hid[span, :] = (pre * sig).astype(BF16)

    store_own(own_s, dot(hid[...], og[...]))
    itself.stage(0)
    r["logits"][...] = (dot_rows(hid[...], r["w2s"][...]) + later).astype(BF16)

    def term(c, block):
        whole = jnp.concatenate([block[0], block[1]], axis=0)
        return lax.dot_general(x[c], whole, (((1,), (1,)), ((), ())), preferred_element_type=F32)

    def sums_on(point):
        for which, number in PLAN[nz].get(point, ()):
            (neigh if which == "n" else itself).stage(number)

    grad = term(z, pg)
    order = [("n", 0)] if near else []
    for s in range(far_r):
        order += [("f", s)] + ([("n", s + 1)] if s + 1 < near else [])
    for j, (kind, s) in enumerate(order):
        pair = ((all_rf, -jump - s), (all_lf, jump + s)) if kind == "f" else ((all_rn, -1 - s), (all_ln, 1 + s))
        pair = [(chain, offset) for chain, offset in pair if s < chain.steps]
        for h in range(2):
            for chain, offset in pair:
                chain.wait_recv(s, h)
                chain.start(s + 1, h)
        for chain, offset in pair:
            grad = grad + term(wrap(z + offset), chain.arrived.at[s])
        sums_on(j)

    own_g, rq, gy, go = r["own_g"], r["g_rq"], r["g_y"], r["g_o"]
    rows_g = own_g.shape[1]
    for j in range(nq):
        own_g[j] = grad[j * rows_g : (j + 1) * rows_g].astype(BF16)
    first = group_q.copies((r["g_s0"], r["g_r0"]), lambda p: own_g.at[p], lambda o: rq.at[o - 1])
    for copy in first:
        copy.start()
    sums_on("a")
    total = own_g[q].astype(F32)
    for o in range(nq - 1):
        first[o].wait_recv()
        total = total + rq[o].astype(F32)
    gy[y] = total.astype(BF16)
    second = group_y.copies((r["g_s1"], r["g_r1"]), lambda p: gy.at[y], lambda o: gy.at[y])
    for copy in second:
        copy.start()
    sums_on("b")
    for chain in (red_rf, red_lf, red_rn, red_ln, all_rf, all_lf, all_rn, all_ln):
        chain.finish()
    neigh.stage(5)
    for copy in second:
        copy.wait_recv()
    total = gy[0].astype(F32)
    for j in range(1, ny):
        total = total + gy[j].astype(F32)
    go[q] = total
    third = group_q.copies((r["g_s2"], r["g_r2"]), lambda p: go.at[q], lambda o: go.at[q])
    for copy in third:
        copy.start()
    sums_on("c")
    itself.stage(5)
    for copy in third:
        copy.wait_recv()
    for j in range(nq):
        r["g1"][j * rows_g : (j + 1) * rows_g, :] = go[j]
    for copies in (first, second, third):
        for copy in copies:
            copy.wait_send()


TOTAL_NAMES = ("rxc", "vy", "ry", "vz", "fy", "fo") + tuple(
    f"{kind}{i}" for i in range(5) for kind in ("s", "r")
)
PLAN = {
    16: {2: ("n1",), 3: ("s1",), 4: ("n2",), 5: ("s2",), "a": ("n3", "s3"), "b": ("n4", "s4")},
    8: {0: ("n1", "s1"), 1: ("n2", "s2"), "a": ("n3", "s3"), "b": ("n4", "s4")},
}
PLAN = {
    size: {point: tuple((stage[0], int(stage[1])) for stage in stages) for point, stages in plan.items()}
    for size, plan in PLAN.items()
}
INPUTS = ("f", "idx", "cnt", "tx", "w1s", "w1n", "hist", "n2", "c2", "og", "w2s", "w2n")


def step(shape, idx, cnt, f, tx, hist, n2, c2, w1s, w1n, og, w2s, w2n):
    nz, ny, nq = shape
    targets, width = og.shape
    half = width // 2
    deep = 2 * tx.shape[0]
    rows_q, rows_y, rows_g = width // nq, width // nq // ny, deep // nq
    jump = nz // 4
    lengths = dict(rf=nz // 2 - jump + 1, lf=nz // 2 - jump, rn=jump - 1, ln=jump - 1)
    V, D = pltpu.VMEM, pltpu.SemaphoreType.DMA
    scratch = dict(
        tab=V((f.shape[1] + 8, 128), F32),
        rows=V((2, 128, 128), F32),
        x=V((nz, deep, 128), BF16),
        w=V((width, deep), BF16),
        agg2=V((width, targets), BF16),
        part=V((nz, width, targets), F32),
        pg=V((2, half, targets), BF16),
        hid=V((width, targets), BF16),
        back=V((width, targets), F32),
        own_n=V((nq, rows_q, width), F32),
        own_s=V((nq, rows_q, width), F32),
        own_g=V((nq, rows_g, width), BF16),
        g_rq=V((nq - 1, rows_g, width), BF16),
        g_y=V((ny, rows_g, width), BF16),
        g_o=V((nq, rows_g, width), F32),
    )
    for i, size in enumerate((nq - 1, ny - 1, nq - 1)):
        scratch[f"g_s{i}"] = D((size,))
        scratch[f"g_r{i}"] = D((size,))
    for name, steps in lengths.items():
        for lead in ("out_", "in_", "ag_"):
            scratch[lead + name] = V((steps, 2, half, targets), BF16)
        for lead in ("rs_s", "rs_r", "ag_s", "ag_r"):
            scratch[lead + name] = D((steps, 2))
    for lead in ("n_", "s_"):
        scratch[lead + "rxc"] = V((nq - 1, rows_q, width), F32)
        scratch[lead + "vy"] = V((ny, rows_y, width), F32)
        scratch[lead + "ry"] = V((ny - 1, rows_y, width), F32)
        scratch[lead + "vz"] = V((nz, rows_y, width), F32)
        scratch[lead + "fy"] = V((ny, rows_y, width), F32)
        scratch[lead + "fo"] = V((nq, ny, rows_y, width), F32)
        for i, size in enumerate((nq, ny, nz, ny, nq)):
            scratch[lead + f"s{i}"] = D((size - 1,))
            scratch[lead + f"r{i}"] = D((size - 1,))
    given = dict(f=f, idx=idx, cnt=cnt, tx=tx, w1s=w1s, w1n=w1n, hist=hist, n2=n2, c2=c2, og=og, w2s=w2s, w2n=w2n)
    for name in INPUTS:
        place = pltpu.SMEM if name == "idx" else V
        scratch["v_" + name] = place(given[name].shape, given[name].dtype)
    scratch["in_sem"] = D((len(INPUTS),))
    names = INPUTS + ("logits", "g1", "gs", "gn") + tuple(scratch)
    vmem = pl.BlockSpec(memory_space=pltpu.VMEM)
    return pl.pallas_call(
        functools.partial(step_kernel, shape, names),
        out_shape=(
            jax.ShapeDtypeStruct((targets, width), BF16),
            jax.ShapeDtypeStruct((deep, width), F32),
            jax.ShapeDtypeStruct((width, width), F32),
            jax.ShapeDtypeStruct((width, width), F32),
        ),
        in_specs=[pl.BlockSpec(memory_space=pl.ANY)] * len(INPUTS),
        out_specs=(vmem,) * 4,
        scratch_shapes=list(scratch.values()),
        compiler_params=pltpu.CompilerParams(
            collective_id=0, has_side_effects=True, vmem_limit_bytes=56 << 20
        ),
    )(*[given[name] for name in INPUTS])


def hand_out_kernel(logits, g1, gs, gn, o0, o1, o2, o3, o4, sems):
    width = o1.shape[0]
    pairs = ((logits, o0), (g1.at[0:width], o1), (g1.at[width : 2 * width], o2), (gs, o3), (gn, o4))
    copies = [pltpu.make_async_copy(a, b, sems.at[i]) for i, (a, b) in enumerate(pairs)]
    for copy in copies:
        copy.start()
    for copy in copies:
        copy.wait()


def hand_out(logits, g1, gs, gn):
    anywhere = pl.BlockSpec(memory_space=pl.ANY)
    like = lambda a: jax.ShapeDtypeStruct(a.shape, a.dtype)
    piece = jax.ShapeDtypeStruct((g1.shape[0] // 2, g1.shape[1]), F32)
    return pl.pallas_call(
        hand_out_kernel,
        out_shape=(like(logits), piece, piece, like(gs), like(gn)),
        in_specs=[anywhere] * 4,
        out_specs=(anywhere,) * 5,
        scratch_shapes=[pltpu.SemaphoreType.DMA((5,))],
        compiler_params=pltpu.CompilerParams(vmem_limit_bytes=56 << 20),
    )(logits, g1, gs, gn)


def local(shape, tx, frontier, n1, c1, w1s, w1n, history, n2, c2, w2s, w2n, og):
    live = lax.broadcasted_iota(jnp.int32, n1.shape, 0) < c1[None, :]
    idx = jnp.where(live, n1, frontier.shape[1]).reshape(-1)
    return hand_out(
        *step(
            shape, idx, c1.reshape(1, -1), frontier, tx, history, n2, c2.reshape(1, -1),
            w1s, w1n, og, w2s, w2n,
        )
    )


SPECS = (
    P("feat", "dp"),
    P("feat", "dp"),
    P(None, "dp"),
    P("dp"),
    P("feat", None),
    P("feat", None),
    P(("dp", "feat"), None),
    P(None, ("dp", "feat")),
    P(("dp", "feat")),
    P(),
    P(),
    P(("dp", "feat"), None),
)


def build(mesh, shape):
    return jax.shard_map(
        functools.partial(local, shape),
        mesh=mesh,
        in_specs=SPECS,
        out_specs=(P(("dp", "feat"), None), P("feat", None), P("feat", None), P(), P()),
        check_vma=False,
    )


def solution(mesh):
    return build(mesh, (mesh.shape["feat"], mesh.shape["dp"] // 8, 8))
```
